256 devices in a mesh: wa: 64 (over z, y, core), col: 4 (over x).
Axes of the slice: x: 4, y: 4, z: 8, core: 2. Of those that a mesh axis runs over, the one named last changes fastest.
Arguments:
- records: float32 [512, 1024, 1024], P('wa', 'col'), as said below
- bin_weight: float32 [128], replicated, may hold values from 0.5 to 2
Outputs:
- coherence: float32 [2, 128, 1024, 1024], P(None, 'wa', 'col')
The draws below stay inside these ranges and needn't reach their ends.
Inputs may be any that keep to these rules, and one draw needn't show every extreme that they name: `records`: finite values.
All inputs are finite; a program needn't handle non-finite values.
Results may differ from the reference program's by a relative error of at most 0.0034.
Values may be sent and summed in bfloat16 or wider, within the bound.
No kernel may reach another device: no remote copies, remote signals or barrier semaphores. Data moves between devices by JAX's collectives and lax.ppermute only.
A program may use at most 64 MiB of HBM per device.

```python
import math
import jax
import jax.numpy as jnp
from jax import lax

C = 1024
S = 1024
K = 128
K0 = 32
W = 512


def draw_records(key, part):
    key = jax.random.fold_in(key, 11)
    keys = jax.random.split(key, 4)
    channel_scale = jnp.exp(jax.random.uniform(keys[0], (C,), jnp.float32, 0.0, math.log(10.0)))
    drift = jax.random.uniform(keys[1], (C,), jnp.float32, -1.0, 1.0)
    window_scale = jnp.exp(jax.random.uniform(keys[2], (W,), jnp.float32, 0.0, math.log(10.0)))
    position = jnp.arange(W, dtype=jnp.float32) / max(W - 1, 1)
    rate = math.log(3.0)
    noise = jax.random.normal(keys[3], (W, C, S), jnp.float32)
    scale = channel_scale[None, :] * jnp.exp(rate * drift[None, :] * position[:, None])
    scale = scale * window_scale[:, None]
    return (noise * scale[:, :, None]).astype(jnp.float32)


def setup_inputs(seed: int = 0) -> dict:
    key_list = jax.random.split(jax.random.key(seed), 3)
    return {
        "records": draw_records(jax.random.fold_in(key_list[2], 71), 0),
        "bin_weight": jnp.clip(jnp.exp(jax.random.uniform(key_list[1], (K,), jnp.float32, math.log(0.5), math.log(2.0))), 0.5, 2.0),
    }


def fourier_table(samples, first_bin, count):
    steps = jnp.arange(samples, dtype=jnp.int32)
    freqs = first_bin + jnp.arange(count, dtype=jnp.int32)
    phases = steps[:, None] * freqs[None, :] % samples
    angles = phases.astype(jnp.float32) * (2.0 * math.pi / samples)
    return jnp.concatenate([jnp.cos(angles), -jnp.sin(angles)], axis=1)

def taper_window(samples):
    steps = jnp.arange(samples, dtype=jnp.int32).astype(jnp.float32)
    return 0.5 - 0.5 * jnp.cos(steps * (2.0 * math.pi / samples))

def reference(records, bin_weight):
    table = fourier_table(S, K0, K)
    tapered = (records * taper_window(S)[None, None, :]).reshape(W * C, S)
    spectra = jnp.dot(tapered, table, precision=lax.Precision.HIGHEST).reshape(W, C, 2 * K)
    real_part = spectra[:, :, :K]
    imag_part = spectra[:, :, K:]
    band_power = lax.optimization_barrier(jnp.sum(real_part * real_part + imag_part * imag_part, axis=1))
    factor = bin_weight[None, :] / jnp.sqrt(band_power / C + 1e-06)
    whitened = (spectra * jnp.concatenate([factor, factor], axis=1)[:, None, :]).astype(jnp.bfloat16)
    squares = whitened.astype(jnp.float32)
    energy = lax.optimization_barrier(jnp.sum(squares * squares, axis=(0, 2)))
    inverse = 1.0 / jnp.sqrt(energy)
    scale = math.sqrt(W) * K
    per_bin = whitened.reshape(W, C, 2, K).transpose(3, 2, 0, 1)

    def one_bin(stacked):
        real_rows = stacked[0].astype(jnp.float32)
        imag_rows = stacked[1].astype(jnp.float32)
        right_side = jnp.concatenate([real_rows, imag_rows], axis=0)
        rotated = jnp.concatenate([imag_rows, -real_rows], axis=0)
        left_side = jnp.concatenate([right_side, rotated], axis=1)
        gram = jnp.dot(left_side.T, right_side, precision=lax.Precision.HIGHEST)
        gram = gram.reshape(2, C, C)
        return gram * (inverse[None, :, None] * inverse[None, None, :] * scale)
    result = lax.map(one_bin, per_bin)
    return result.transpose(1, 0, 2, 3)
```

```python
import functools
import math

import jax
import jax.numpy as jnp
import numpy as np
from jax import lax
from jax.experimental import pallas as pl
from jax.experimental.pallas import tpu as pltpu
from jax.sharding import PartitionSpec as P

K0 = 32
BF = jnp.bfloat16
F32 = jnp.float32


def split_tables(samples, kept):
    half = samples // 2
    steps = np.arange(half, dtype=np.int64)
    tables = []
    for parity in range(2):
        freqs = K0 + np.arange(parity, kept, 2)
        angles = 2.0 * math.pi / samples * ((steps[None, :] * freqs[:, None]) % samples)
        exact = np.concatenate([np.cos(angles), -np.sin(angles)], axis=0).astype(np.float32)
        high = exact.astype(BF)
        low = (exact - high.astype(np.float32)).astype(BF)
        tables.append(np.concatenate([high, low], axis=0))
    return np.stack(tables)


def taper_window(samples):
    steps = np.arange(samples)
    return (0.5 - 0.5 * np.cos(2.0 * math.pi / samples * steps)).astype(np.float32)[None, :]


def nt(a, b):
    return lax.dot_general(a, b, (((1,), (1,)), ((), ())), preferred_element_type=F32)


def spectra_kernel(records, taper, tables, spec, power):
    w = pl.program_id(0)
    samples = records.shape[2]
    half = samples // 2
    bins = tables.shape[1] // 4
    tapered = records[0] * taper[...]
    first, second = tapered[:, :half], tapered[:, half:]
    ones = jnp.ones((8, records.shape[1]), BF)
    rows = []
    for parity in range(2):
        folded = first + second if parity == 0 else first - second
        high = folded.astype(BF)
        low = (folded - high.astype(F32)).astype(BF)
        both = nt(tables[parity], high)
        result = both[: 2 * bins] + both[2 * bins :] + nt(tables[parity, : 2 * bins], low)
        real, imag = result[:bins], result[bins:]
        for side in range(2):
            lanes = slice(128 * side, 128 * side + 128)
            spec[side, pl.ds(16 * parity + w, bins, stride=32), :] = real[:, lanes]
            spec[side, pl.ds(16 * parity + 8 + w, bins, stride=32), :] = imag[:, lanes]
        square = real * real + imag * imag
        top = square.astype(BF)
        rest = square - top.astype(F32)
        mid = rest.astype(BF)
        end = (rest - mid.astype(F32)).astype(BF)
        rows.append(nt(ones, top) + nt(ones, mid) + nt(ones, end))
    power[pl.ds(w, 1), :] = jnp.concatenate(rows, axis=1)[:1]


def whiten_kernel(channels, spec, power, weight, message):
    bins = power.shape[1] // 2
    factor = weight[...] / jnp.sqrt(power[...] / channels + 1e-06)
    energy = jnp.zeros((8, 256), F32)
    for owner in range(bins):
        for parity in range(2):
            lane = parity * bins + owner
            scale = factor[:, lane : lane + 1]
            start = owner * 32 + parity * 16
            block = jnp.concatenate(
                [spec[0, start : start + 16, :], spec[1, start : start + 16, :]], axis=1
            )
            real = (block[:8] * scale).astype(BF).astype(F32)
            imag = (block[8:] * scale).astype(BF).astype(F32)
            energy = energy + (real * real + imag * imag)
            message[owner, 16 * parity : 16 * parity + 16, :] = jnp.concatenate(
                [real, imag], axis=0
            ).astype(BF)
    total = jnp.sum(energy, axis=0, keepdims=True)
    high = total.astype(BF).astype(F32)
    mid = (total - high).astype(BF).astype(F32)
    low = total - high - mid
    row = lax.broadcasted_iota(jnp.int32, (8, 256), 0)
    tail = jnp.where(row == 0, high, jnp.where(row == 1, mid, jnp.where(row == 2, low, 0.0)))
    tail = tail.astype(BF)
    for owner in range(bins):
        message[owner, 32:40, :] = tail


def gram_kernel(scale, col, own, right, left, far_a, far_b, energy, out, lhs):
    step = pl.program_id(1)
    depth = own.shape[0] * own.shape[1]
    chan = own.shape[2]
    half = depth // 2
    me = col[0]

    def emit(product, which):
        rows = lax.rsqrt(energy[0:1, :]) * scale
        cols = lax.rsqrt(energy[pl.ds(which, 1), :])
        weight = jnp.transpose(jnp.broadcast_to(rows, (8, chan)))[:, :1] * cols
        out[0, 0] = product[:chan] * weight
        out[1, 0] = product[chan:] * weight

    @pl.when(step == 0)
    def _():
        mine = own[...].reshape(depth, chan)
        real = own[:, :8, :]
        turned = jnp.concatenate([own[:, 8:, :], -real], axis=1).reshape(depth, chan)
        lhs[:chan] = jnp.transpose(mine)
        lhs[chan:] = jnp.transpose(turned)
        emit(jnp.dot(lhs[...], mine, preferred_element_type=F32), 0)

    @pl.when(step == 1)
    def _():
        emit(jnp.dot(lhs[...], right[...].reshape(depth, chan), preferred_element_type=F32), 1)

    @pl.when(step == 2)
    def _():
        emit(jnp.dot(lhs[...], left[...].reshape(depth, chan), preferred_element_type=F32), 2)

    @pl.when(step == 3)
    def _():
        product = jnp.dot(
            lhs[:, :half], far_a[...].reshape(half, chan), preferred_element_type=F32
        )
        product += jnp.dot(
            lhs[:, half:], far_b[...].reshape(half, chan), preferred_element_type=F32
        )
        emit(product, 3)


def ring(size, shift):
    return [(i, (i + shift) % size) for i in range(size)]


def body(owners, columns, records, bin_weight):
    windows, chan, samples = records.shape
    kept = bin_weight.shape[0]
    bins = kept // 2
    spec, power = pl.pallas_call(
        spectra_kernel,
        grid=(windows,),
        in_specs=[
            pl.BlockSpec((1, chan, samples), lambda w: (w, 0, 0)),
            pl.BlockSpec((1, samples), lambda w: (0, 0)),
            pl.BlockSpec((2, 2 * kept, samples // 2), lambda w: (0, 0, 0)),
        ],
        out_specs=[
            pl.BlockSpec((2, kept * 16, 128), lambda w: (0, 0, 0)),
            pl.BlockSpec((windows, kept), lambda w: (0, 0)),
        ],
        out_shape=[
            jax.ShapeDtypeStruct((2, kept * 16, 128), F32),
            jax.ShapeDtypeStruct((windows, kept), F32),
        ],
        compiler_params=pltpu.CompilerParams(vmem_limit_bytes=58 << 20),
        name="spectra",
    )(records, taper_window(samples), split_tables(samples, kept))
    power = lax.psum(power, "col")
    weight = bin_weight.reshape(bins, 2).T.reshape(1, kept)
    message = pl.pallas_call(
        functools.partial(whiten_kernel, chan * columns),
        out_shape=jax.ShapeDtypeStruct((owners, 40, chan), BF),
        compiler_params=pltpu.CompilerParams(vmem_limit_bytes=40 << 20),
        name="whiten",
    )(spec, power, weight)
    owned = lax.all_to_all(message, "wa", split_axis=0, concat_axis=0, tiled=True)
    mine = owned[:, :32]
    energy = jnp.sum(owned[:, 32:].astype(F32), axis=(0, 1))[None, :]
    ahead, back = ring(columns, 1), ring(columns, columns - 1)
    from_left = lax.ppermute(mine, "col", ahead)
    from_right = lax.ppermute(mine, "col", back)
    half = owners // 2
    far_a = lax.ppermute(from_left[:half], "col", ahead)
    far_b = lax.ppermute(from_right[half:], "col", back)
    energies = jnp.concatenate(
        [
            energy,
            lax.ppermute(energy, "col", back),
            lax.ppermute(energy, "col", ahead),
            lax.ppermute(energy, "col", ring(columns, 2)),
        ],
        axis=0,
    )
    col = lax.axis_index("col").astype(jnp.int32)[None]
    total_windows = windows * owners
    scale = math.sqrt(total_windows) * kept

    def where(b, s, c):
        shift = jnp.where(s == 2, 3, jnp.where(s == 3, 2, s))
        return (0, b, 0, lax.rem(c[0] + shift, columns))

    bin_block = lambda n: pl.BlockSpec((n, 16, chan), lambda b, s, c: (0, b, 0))
    return pl.pallas_call(
        functools.partial(gram_kernel, scale),
        grid_spec=pltpu.PrefetchScalarGridSpec(
            num_scalar_prefetch=1,
            grid=(2, 4),
            in_specs=[
                bin_block(owners),
                bin_block(owners),
                bin_block(owners),
                bin_block(half),
                bin_block(half),
                pl.BlockSpec((4, chan), lambda b, s, c: (0, 0)),
            ],
            out_specs=pl.BlockSpec((2, 1, chan, chan), where),
            scratch_shapes=[pltpu.VMEM((2 * chan, 16 * owners), BF)],
        ),
        out_shape=jax.ShapeDtypeStruct((2, 2, chan, chan * columns), F32),
        compiler_params=pltpu.CompilerParams(vmem_limit_bytes=40 << 20),
        name="gram",
    )(col, mine, from_right, from_left, far_a, far_b, energies)


def solution(mesh):
    owners, columns = mesh.shape["wa"], mesh.shape["col"]
    return jax.shard_map(
        functools.partial(body, owners, columns),
        mesh=mesh,
        in_specs=(P("wa", "col", None), P()),
        out_specs=P(None, "wa", "col", None),
        check_vma=False,
    )
```

```python
import functools
import math

import jax
import jax.numpy as jnp
import numpy as np
from jax import lax
from jax.experimental import pallas as pl
from jax.experimental.pallas import tpu as pltpu
from jax.sharding import PartitionSpec as P

K0 = 32
BF = jnp.bfloat16
F32 = jnp.float32


def split_tables(samples, kept):
    half = samples // 2
    steps = np.arange(half, dtype=np.int64)
    tables = []
    for parity in range(2):
        freqs = K0 + np.arange(parity, kept, 2)
        angles = 2.0 * math.pi / samples * ((steps[:, None] * freqs[None, :]) % samples)
        exact = np.concatenate([np.cos(angles), -np.sin(angles)], axis=1).astype(np.float32)
        high = exact.astype(BF)
        low = (exact - high.astype(np.float32)).astype(BF)
        tables.append(np.concatenate([high, low], axis=1))
    return np.stack(tables)


def taper_window(samples):
    steps = np.arange(samples)
    return (0.5 - 0.5 * np.cos(2.0 * math.pi / samples * steps)).astype(np.float32)[None, :]


def dot(a, b):
    return jnp.dot(a, b, preferred_element_type=F32)


def spectra_kernel(records, taper, tables, even, odd, power, held, arrived):
    windows = records.shape[0]
    half = records.shape[2] // 2
    kept = tables.shape[2] // 2
    bins = kept // 2

    def fetch(w):
        return pltpu.make_async_copy(records.at[w], held.at[w], arrived.at[w])

    for w in range(windows):
        fetch(w).start()

    @pl.loop(0, windows)
    def _(w):
        fetch(w).wait()
        tapered = held[w] * taper[...]
        first, second = tapered[:, :half], tapered[:, half:]
        rows = []
        for parity, spec in enumerate((even, odd)):
            folded = first + second if parity == 0 else first - second
            high = folded.astype(BF)
            low = (folded - high.astype(F32)).astype(BF)
            both = dot(high, tables[parity])
            result = both[:, :kept] + both[:, kept:] + dot(low, tables[parity, :, :kept])
            square = jnp.sum(result * result, axis=0, keepdims=True)
            rows.append(square[:, :bins] + square[:, bins:])
            turned = jnp.transpose(result)
            for side in range(2):
                lanes = slice(128 * side, 128 * side + 128)
                spec[side, pl.ds(w, bins, stride=16), :] = turned[:bins, lanes]
                spec[side, pl.ds(8 + w, bins, stride=16), :] = turned[bins:, lanes]
        power[pl.ds(w, 1), :] = jnp.concatenate(rows, axis=1)


def whiten_kernel(channels, even, odd, p0, p1, p2, p3, weight, message, energy):
    bins = p0.shape[1] // 2
    power = (p0[...] + p1[...]) + (p2[...] + p3[...])
    factor = weight[...] / jnp.sqrt(power / channels + 1e-06)
    total = jnp.zeros((8, 256), F32)
    for owner in range(bins):
        for parity, spec in enumerate((even, odd)):
            lane = parity * bins + owner
            scale = factor[:, lane : lane + 1]
            start = owner * 16
            block = jnp.concatenate(
                [spec[0, start : start + 16, :], spec[1, start : start + 16, :]], axis=1
            )
            real = (block[:8] * scale).astype(BF).astype(F32)
            imag = (block[8:] * scale).astype(BF).astype(F32)
            total = total + (real * real + imag * imag)
            message[owner, parity * 16 : parity * 16 + 16, :] = jnp.concatenate(
                [real, imag], axis=0
            ).astype(BF)
    energy[...] = jnp.sum(total, axis=0, keepdims=True)


def flat(block):
    return block.reshape(block.shape[0] * block.shape[1], block.shape[2])


def left_side(own, lhs):
    chan = own.shape[2]
    turned = jnp.concatenate([own[:, 8:, :], -own[:, :8, :]], axis=1)
    lhs[:chan] = jnp.transpose(flat(own[...]))
    lhs[chan:] = jnp.transpose(flat(turned))


def emit(product, energy, which, scale, out):
    chan = product.shape[1]
    rows = lax.rsqrt(energy[0:1, :]) * scale
    cols = lax.rsqrt(energy[pl.ds(which, 1), :])
    weight = jnp.transpose(jnp.broadcast_to(rows, (8, chan)))[:, :1] * cols
    out[0, 0] = product[:chan] * weight
    out[1, 0] = product[chan:] * weight


def gram_near_kernel(scale, col, own, right_a, right_b, left_a, left_b, energy, out, lhs):
    step = pl.program_id(1)
    half = lhs.shape[2] // 2

    @pl.when(step == 0)
    def _():
        left_side(own, lhs.at[0])
        emit(dot(lhs[0], flat(own[...])), energy, 0, scale, out)

    for which, first, second in ((1, right_a, right_b), (2, left_a, left_b)):

        @pl.when(step == which)
        def _():
            product = dot(lhs[0, :, :half], flat(first[...]))
            product += dot(lhs[0, :, half:], flat(second[...]))
            emit(product, energy, which, scale, out)


def gram_far_kernel(scale, col, lhs, far_a, far_b, energy, kept, out):
    half = lhs.shape[2] // 2
    product = dot(lhs[0, :, :half], flat(far_a[...])) + dot(lhs[0, :, half:], flat(far_b[...]))
    emit(product, energy, 3, scale, out)


def ring(size, shift):
    return [(i, (i + shift) % size) for i in range(size)]


def body(owners, columns, records, bin_weight):
    windows, chan, samples = records.shape
    kept = bin_weight.shape[0]
    bins = kept // 2
    spec_shape = (2, bins * 16, 128)
    even, odd, power = pl.pallas_call(
        spectra_kernel,
        in_specs=[
            pl.BlockSpec(memory_space=pltpu.HBM),
            pl.BlockSpec(memory_space=pltpu.VMEM),
            pl.BlockSpec(memory_space=pltpu.VMEM),
        ],
        scratch_shapes=[
            pltpu.VMEM((windows, chan, samples), F32),
            pltpu.SemaphoreType.DMA((windows,)),
        ],
        out_shape=[
            jax.ShapeDtypeStruct(spec_shape, F32),
            jax.ShapeDtypeStruct(spec_shape, F32),
            jax.ShapeDtypeStruct((windows, kept), F32),
        ],
        compiler_params=pltpu.CompilerParams(vmem_limit_bytes=50 << 20),
        name="spectra",
    )(records, taper_window(samples), split_tables(samples, kept))
    ahead, back, across = ring(columns, 1), ring(columns, columns - 1), ring(columns, 2)
    powers = [power] + [lax.ppermute(power, "col", p) for p in (ahead, back, across)]
    weight = bin_weight.reshape(bins, 2).T.reshape(1, kept)
    message, energy = pl.pallas_call(
        functools.partial(whiten_kernel, chan * columns),
        out_shape=[
            jax.ShapeDtypeStruct((owners, 32, chan), BF),
            jax.ShapeDtypeStruct((1, chan), F32),
        ],
        compiler_params=pltpu.CompilerParams(vmem_limit_bytes=10 << 20),
        name="whiten",
    )(even, odd, *powers, weight)

    mine = lax.all_to_all(message, "wa", split_axis=0, concat_axis=0, tiled=True)
    energies = jnp.concatenate(
        [energy] + [lax.ppermute(energy, "col", p) for p in (back, ahead, across)], axis=0
    )

    def fold(value, step):
        return value + lax.ppermute(value, "wa", [(i, i ^ step) for i in range(owners)])

    for step in (1, 2, 4):
        energies = fold(energies, step)
    mine, energies = lax.optimization_barrier((mine, energies))

    half = owners // 2
    left_a = lax.ppermute(mine[:half], "col", ahead)
    right_b = lax.ppermute(mine[half:], "col", back)
    energies = fold(fold(energies, 8), 16)
    mine, left_a, right_b, energies = lax.optimization_barrier(
        (mine, left_a, right_b, energies)
    )
    left_b = lax.ppermute(mine[half:], "col", ahead)
    right_a = lax.ppermute(mine[:half], "col", back)
    far_a = lax.ppermute(left_a, "col", ahead)
    far_b = lax.ppermute(right_b, "col", back)
    energies = fold(energies, 32)

    col = lax.axis_index("col").astype(jnp.int32)[None]
    scale = math.sqrt(windows * owners) * kept
    out_shape = jax.ShapeDtypeStruct((2, 2, chan, chan * columns), F32)
    lhs_shape = (2, 2 * chan, 16 * owners)

    def where(s, c):
        shift = jnp.where(s == 2, 3, jnp.where(s == 3, 2, s))
        return lax.rem(c[0] + shift, columns)

    def bin_block(count):
        return pl.BlockSpec((count, 16, chan), lambda b, s, c: (0, b, 0))

    def out_block(first):
        return pl.BlockSpec((2, 1, chan, chan), lambda b, s, c: (0, b, 0, where(s + first, c)))

    energy_block = pl.BlockSpec((columns, chan), lambda b, s, c: (0, 0))
    lhs_block = pl.BlockSpec((1,) + lhs_shape[1:], lambda b, s, c: (b, 0, 0))
    params = pltpu.CompilerParams(vmem_limit_bytes=16 << 20)
    out, lhs = pl.pallas_call(
        functools.partial(gram_near_kernel, scale),
        grid_spec=pltpu.PrefetchScalarGridSpec(
            num_scalar_prefetch=1,
            grid=(2, 3),
            in_specs=[bin_block(owners)] + [bin_block(half)] * 4 + [energy_block],
            out_specs=[out_block(0), lhs_block],
        ),
        out_shape=[out_shape, jax.ShapeDtypeStruct(lhs_shape, BF)],
        compiler_params=params,
        cost_estimate=pl.CostEstimate(
            flops=24 * chan * chan * 16 * owners, bytes_accessed=8 << 20, transcendentals=0
        ),
        name="gram_near",
    )(col, mine, right_a, right_b, left_a, left_b, energies)
    return pl.pallas_call(
        functools.partial(gram_far_kernel, scale),
        grid_spec=pltpu.PrefetchScalarGridSpec(
            num_scalar_prefetch=1,
            grid=(2, 1),
            in_specs=[lhs_block, bin_block(half), bin_block(half), energy_block]
            + [pl.BlockSpec(memory_space=pl.ANY)],
            out_specs=out_block(3),
        ),
        out_shape=out_shape,
        input_output_aliases={5: 0},
        compiler_params=params,
        cost_estimate=pl.CostEstimate(
            flops=8 * chan * chan * 16 * owners, bytes_accessed=4 << 20, transcendentals=0
        ),
        name="gram_far",
    )(col, lhs, far_a, far_b, energies, out)


def solution(mesh):
    owners, columns = mesh.shape["wa"], mesh.shape["col"]
    return jax.shard_map(
        functools.partial(body, owners, columns),
        mesh=mesh,
        in_specs=(P("wa", "col", None), P()),
        out_specs=P(None, "wa", "col", None),
        check_vma=False,
    )
```

```python
import functools
import math

import jax
import jax.numpy as jnp
import numpy as np
from jax import lax
from jax.experimental import pallas as pl
from jax.experimental.pallas import tpu as pltpu
from jax.sharding import PartitionSpec as P

K0 = 32
BF = jnp.bfloat16
F32 = jnp.float32


def split_tables(samples, kept):
    half = samples // 2
    steps = np.arange(half, dtype=np.int64)
    tables = []
    for parity in range(2):
        freqs = K0 + np.arange(parity, kept, 2)
        angles = 2.0 * math.pi / samples * ((steps[:, None] * freqs[None, :]) % samples)
        exact = np.concatenate([np.cos(angles), -np.sin(angles)], axis=1).astype(np.float32)
        high = exact.astype(BF)
        low = (exact - high.astype(np.float32)).astype(BF)
        tables.append(np.concatenate([high, low], axis=1))
    return np.stack(tables)


def dot(a, b):
    return jnp.dot(a, b, preferred_element_type=F32)


def spectra_kernel(records, tables, even, odd, power, held, results, arrived):
    windows, _, samples = records.shape
    half = samples // 2
    kept = tables.shape[2] // 2
    bins = kept // 2

    def fetch(w):
        return pltpu.make_async_copy(records.at[w], held.at[w], arrived.at[w])

    for w in range(windows):
        fetch(w).start()
    steps = lax.broadcasted_iota(jnp.int32, (1, samples), 1).astype(F32)
    taper = 0.5 - 0.5 * jnp.cos(steps * (2.0 * math.pi / samples))

    for w in range(windows + 1):
        if w < windows:
            fetch(w).wait()
            tapered = held[w] * taper
            first, second = tapered[:, :half], tapered[:, half:]
            rows = []
            for parity in range(2):
                folded = first + second if parity == 0 else first - second
                high = folded.astype(BF)
                low = (folded - high.astype(F32)).astype(BF)
                both = dot(high, tables[parity])
                result = both[:, :kept] + both[:, kept:] + dot(low, tables[parity, :, :kept])
                results[w % 2, parity] = result
                square = jnp.sum(result * result, axis=0, keepdims=True)
                rows.append(square[:, :bins] + square[:, bins:])
            power[w : w + 1, :] = jnp.concatenate(rows, axis=1)
        if w > 0:
            for parity, spec in enumerate((even, odd)):
                turned = jnp.transpose(results[(w - 1) % 2, parity])
                for side in range(2):
                    lanes = slice(128 * side, 128 * side + 128)
                    spec[side, pl.ds(w - 1, bins, stride=16), :] = turned[:bins, lanes]
                    spec[side, pl.ds(7 + w, bins, stride=16), :] = turned[bins:, lanes]


def whiten_kernel(channels, even, odd, p0, p1, p2, p3, weight, message, energy):
    bins = p0.shape[1] // 2
    power = (p0[...] + p1[...]) + (p2[...] + p3[...])
    factor = weight[...] / jnp.sqrt(power / channels + 1e-06)
    total = jnp.zeros((8, 256), F32)
    for owner in range(bins):
        for parity, spec in enumerate((even, odd)):
            lane = parity * bins + owner
            scale = factor[:, lane : lane + 1]
            start = owner * 16
            block = jnp.concatenate(
                [spec[0, start : start + 16, :], spec[1, start : start + 16, :]], axis=1
            )
            real = (block[:8] * scale).astype(BF).astype(F32)
            imag = (block[8:] * scale).astype(BF).astype(F32)
            total = total + (real * real + imag * imag)
            message[owner, parity * 16 : parity * 16 + 16, :] = jnp.concatenate(
                [real, imag], axis=0
            ).astype(BF)
    energy[...] = jnp.sum(total, axis=0, keepdims=True)


def flat(block):
    return block.reshape(block.shape[0] * block.shape[1], block.shape[2])


def left_side(own, lhs):
    chan = own.shape[2]
    turned = jnp.concatenate([own[:, 8:, :], -own[:, :8, :]], axis=1)
    lhs[:chan] = jnp.transpose(flat(own[...]))
    lhs[chan:] = jnp.transpose(flat(turned))


def emit(product, energy, which, scale, out):
    chan = product.shape[1]
    rows = lax.rsqrt(energy[0:1, :]) * scale
    cols = lax.rsqrt(energy[pl.ds(which, 1), :])
    weight = jnp.transpose(jnp.broadcast_to(rows, (8, chan)))[:, :1] * cols
    out[0, 0] = product[:chan] * weight
    out[1, 0] = product[chan:] * weight


def gram_near_kernel(scale, col, own, right_a, right_b, left_a, left_b, energy, out, lhs):
    step = pl.program_id(1)
    half = lhs.shape[2] // 2

    @pl.when(step == 0)
    def _():
        left_side(own, lhs.at[0])
        emit(dot(lhs[0], flat(own[...])), energy, 0, scale, out)

    for which, first, second in ((1, right_a, right_b), (2, left_a, left_b)):

        @pl.when(step == which)
        def _():
            product = dot(lhs[0, :, :half], flat(first[...]))
            product += dot(lhs[0, :, half:], flat(second[...]))
            emit(product, energy, which, scale, out)


def gram_far_kernel(scale, col, lhs, far_a, far_b, energy, kept, out):
    half = lhs.shape[2] // 2
    product = dot(lhs[0, :, :half], flat(far_a[...])) + dot(lhs[0, :, half:], flat(far_b[...]))
    emit(product, energy, 3, scale, out)


def ring(size, shift):
    return [(i, (i + shift) % size) for i in range(size)]


def body(owners, columns, records, bin_weight):
    windows, chan, samples = records.shape
    kept = bin_weight.shape[0]
    bins = kept // 2
    spec_shape = (2, bins * 16, 128)
    even, odd, power = pl.pallas_call(
        spectra_kernel,
        in_specs=[
            pl.BlockSpec(memory_space=pltpu.HBM),
            pl.BlockSpec(memory_space=pltpu.VMEM),
        ],
        out_shape=[
            jax.ShapeDtypeStruct(spec_shape, F32),
            jax.ShapeDtypeStruct(spec_shape, F32),
            jax.ShapeDtypeStruct((windows, kept), F32),
        ],
        scratch_shapes=[
            pltpu.VMEM((windows, chan, samples), F32),
            pltpu.VMEM((2, 2, chan, kept), F32),
            pltpu.SemaphoreType.DMA((windows,)),
        ],
        compiler_params=pltpu.CompilerParams(vmem_limit_bytes=50 << 20),
        name="spectra",
    )(records, split_tables(samples, kept))
    ahead, back, across = ring(columns, 1), ring(columns, columns - 1), ring(columns, 2)
    powers = [power] + [lax.ppermute(power, "col", p) for p in (ahead, back, across)]
    weight = bin_weight.reshape(bins, 2).T.reshape(1, kept)
    message, energy = pl.pallas_call(
        functools.partial(whiten_kernel, chan * columns),
        out_shape=[
            jax.ShapeDtypeStruct((owners, 32, chan), BF),
            jax.ShapeDtypeStruct((1, chan), F32),
        ],
        compiler_params=pltpu.CompilerParams(vmem_limit_bytes=10 << 20),
        name="whiten",
    )(even, odd, *powers, weight)

    mine = lax.all_to_all(message, "wa", split_axis=0, concat_axis=0, tiled=True)
    energies = jnp.concatenate(
        [energy] + [lax.ppermute(energy, "col", p) for p in (back, ahead, across)], axis=0
    )

    def fold(value, step):
        return value + lax.ppermute(value, "wa", [(i, i ^ step) for i in range(owners)])

    for step in (1, 2, 4):
        energies = fold(energies, step)
    mine, energies = lax.optimization_barrier((mine, energies))

    half = owners // 2
    left_a = lax.ppermute(mine[:half], "col", ahead)
    right_b = lax.ppermute(mine[half:], "col", back)
    left_b = lax.ppermute(mine[half:], "col", ahead)
    right_a = lax.ppermute(mine[:half], "col", back)
    energies = fold(fold(energies, 8), 16)
    left_a, right_b, energies = lax.optimization_barrier((left_a, right_b, energies))
    far_a = lax.ppermute(left_a, "col", ahead)
    far_b = lax.ppermute(right_b, "col", back)
    energies = fold(energies, 32)

    col = lax.axis_index("col").astype(jnp.int32)[None]
    scale = math.sqrt(windows * owners) * kept
    out_shape = jax.ShapeDtypeStruct((2, 2, chan, chan * columns), F32)
    lhs_shape = (2, 2 * chan, 16 * owners)

    def where(s, c):
        shift = jnp.where(s == 2, 3, jnp.where(s == 3, 2, s))
        return lax.rem(c[0] + shift, columns)

    def bin_block(count):
        return pl.BlockSpec((count, 16, chan), lambda b, s, c: (0, b, 0))

    def out_block(first):
        return pl.BlockSpec((2, 1, chan, chan), lambda b, s, c: (0, b, 0, where(s + first, c)))

    energy_block = pl.BlockSpec((columns, chan), lambda b, s, c: (0, 0))
    lhs_block = pl.BlockSpec((1,) + lhs_shape[1:], lambda b, s, c: (b, 0, 0))
    params = pltpu.CompilerParams(vmem_limit_bytes=16 << 20)
    out, lhs = pl.pallas_call(
        functools.partial(gram_near_kernel, scale),
        grid_spec=pltpu.PrefetchScalarGridSpec(
            num_scalar_prefetch=1,
            grid=(2, 3),
            in_specs=[bin_block(owners)] + [bin_block(half)] * 4 + [energy_block],
            out_specs=[out_block(0), lhs_block],
        ),
        out_shape=[out_shape, jax.ShapeDtypeStruct(lhs_shape, BF)],
        compiler_params=params,
        cost_estimate=pl.CostEstimate(
            flops=24 * chan * chan * 16 * owners, bytes_accessed=8 << 20, transcendentals=0
        ),
        name="gram_near",
    )(col, mine, right_a, right_b, left_a, left_b, energies)
    return pl.pallas_call(
        functools.partial(gram_far_kernel, scale),
        grid_spec=pltpu.PrefetchScalarGridSpec(
            num_scalar_prefetch=1,
            grid=(2, 1),
            in_specs=[lhs_block, bin_block(half), bin_block(half), energy_block]
            + [pl.BlockSpec(memory_space=pl.ANY)],
            out_specs=out_block(3),
        ),
        out_shape=out_shape,
        input_output_aliases={5: 0},
        compiler_params=params,
        cost_estimate=pl.CostEstimate(
            flops=8 * chan * chan * 16 * owners, bytes_accessed=4 << 20, transcendentals=0
        ),
        name="gram_far",
    )(col, lhs, far_a, far_b, energies, out)


def solution(mesh):
    owners, columns = mesh.shape["wa"], mesh.shape["col"]
    return jax.shard_map(
        functools.partial(body, owners, columns),
        mesh=mesh,
        in_specs=(P("wa", "col", None), P()),
        out_specs=P(None, "wa", "col", None),
        check_vma=False,
    )
```

```python
import functools
import math

import jax
import jax.numpy as jnp
import numpy as np
from jax import lax
from jax.experimental import pallas as pl
from jax.experimental.pallas import tpu as pltpu
from jax.sharding import PartitionSpec as P

K0 = 32
BF = jnp.bfloat16
F32 = jnp.float32


def split_tables(samples, kept):
    half = samples // 2
    steps = np.arange(half, dtype=np.int64)
    tables = []
    for parity in range(2):
        freqs = K0 + np.arange(parity, kept, 2)
        angles = 2.0 * math.pi / samples * ((steps[:, None] * freqs[None, :]) % samples)
        exact = np.concatenate([np.cos(angles), -np.sin(angles)], axis=1).astype(np.float32)
        high = exact.astype(BF)
        low = (exact - high.astype(np.float32)).astype(BF)
        tables.append(np.concatenate([high, low], axis=1))
    return np.stack(tables)


def dot(a, b):
    return jnp.dot(a, b, preferred_element_type=F32)


def spectra_kernel(records, tables, even, odd, power, held, results, arrived):
    windows, _, samples = records.shape
    half = samples // 2
    kept = tables.shape[2] // 2
    bins = kept // 2

    def fetch(w):
        return pltpu.make_async_copy(records.at[w], held.at[w], arrived.at[w])

    for w in range(windows):
        fetch(w).start()
    steps = lax.broadcasted_iota(jnp.int32, (1, samples), 1).astype(F32)
    taper = 0.5 - 0.5 * jnp.cos(steps * (2.0 * math.pi / samples))

    chan = records.shape[1]
    for pair in range(0, windows + 2, 2):
        if pair < windows:
            fetch(pair).wait()
            fetch(pair + 1).wait()
            tapered = held[pair : pair + 2].reshape(2 * chan, samples) * taper
            first, second = tapered[:, :half], tapered[:, half:]
            rows = [[], []]
            for parity in range(2):
                folded = first + second if parity == 0 else first - second
                high = folded.astype(BF)
                low = (folded - high.astype(F32)).astype(BF)
                both = dot(high, tables[parity])
                result = both[:, :kept] + both[:, kept:] + dot(low, tables[parity, :, :kept])
                square = result * result
                for i in range(2):
                    part = slice(i * chan, i * chan + chan)
                    results[pair + i, parity] = result[part]
                    total = jnp.sum(square[part], axis=0, keepdims=True)
                    rows[i].append(total[:, :bins] + total[:, bins:])
            for i in range(2):
                power[pair + i : pair + i + 1, :] = jnp.concatenate(rows[i], axis=1)
        for w in range(pair - 2, pair) if pair else ():
            for parity, spec in enumerate((even, odd)):
                turned = jnp.transpose(results[w, parity])
                for side in range(2):
                    lanes = slice(128 * side, 128 * side + 128)
                    spec[side, pl.ds(w, bins, stride=16), :] = turned[:bins, lanes]
                    spec[side, pl.ds(8 + w, bins, stride=16), :] = turned[bins:, lanes]


def whiten_kernel(channels, even, odd, p0, p1, p2, p3, weight, message, energy, held, sent):
    bins = p0.shape[1] // 2
    group = bins // 4
    power = (p0[...] + p1[...]) + (p2[...] + p3[...])
    factor = weight[...] / jnp.sqrt(power / channels + 1e-06)
    total = jnp.zeros((8, 256), F32)

    def send(part):
        owners = pl.ds(part * group, group)
        return pltpu.make_async_copy(held.at[owners], message.at[owners], sent.at[part])

    for owner in range(bins):
        for parity, spec in enumerate((even, odd)):
            lane = parity * bins + owner
            scale = factor[:, lane : lane + 1]
            start = owner * 16
            block = jnp.concatenate(
                [spec[0, start : start + 16, :], spec[1, start : start + 16, :]], axis=1
            )
            real = (block[:8] * scale).astype(BF).astype(F32)
            imag = (block[8:] * scale).astype(BF).astype(F32)
            total = total + (real * real + imag * imag)
            held[owner, parity * 16 : parity * 16 + 16, :] = jnp.concatenate(
                [real, imag], axis=0
            ).astype(BF)
        if owner % group == group - 1:
            send(owner // group).start()
    energy[...] = jnp.sum(total, axis=0, keepdims=True)
    for part in range(4):
        send(part).wait()


def flat(block):
    return block.reshape(block.shape[0] * block.shape[1], block.shape[2])


def left_side(own, lhs):
    chan = own.shape[2]
    turned = jnp.concatenate([own[:, 8:, :], -own[:, :8, :]], axis=1)
    lhs[:chan] = jnp.transpose(flat(own[...]))
    lhs[chan:] = jnp.transpose(flat(turned))


def emit(product, energy, which, scale, out):
    chan = product.shape[1]
    rows = lax.rsqrt(energy[0:1, :]) * scale
    cols = lax.rsqrt(energy[pl.ds(which, 1), :])
    weight = jnp.transpose(jnp.broadcast_to(rows, (8, chan)))[:, :1] * cols
    out[0, 0] = product[:chan] * weight
    out[1, 0] = product[chan:] * weight


def gram_near_kernel(scale, col, own, right_a, right_b, left_a, left_b, energy, out, lhs):
    step = pl.program_id(1)
    half = lhs.shape[2] // 2

    @pl.when(step == 0)
    def _():
        left_side(own, lhs.at[0])
        emit(dot(lhs[0], flat(own[...])), energy, 0, scale, out)

    for which, first, second in ((1, right_a, right_b), (2, left_a, left_b)):

        @pl.when(step == which)
        def _():
            product = dot(lhs[0, :, :half], flat(first[...]))
            product += dot(lhs[0, :, half:], flat(second[...]))
            emit(product, energy, which, scale, out)


def gram_far_kernel(scale, col, lhs, far_a, far_b, energy, kept, out):
    half = lhs.shape[2] // 2
    b = pl.program_id(0)
    rows = pl.ds(pl.multiple_of(b * 16, 16), 16)
    product = dot(lhs[b, :, :half], flat(far_a[:, rows, :]))
    product += dot(lhs[b, :, half:], flat(far_b[:, rows, :]))
    emit(product, energy, 3, scale, out)


def ring(size, shift):
    return [(i, (i + shift) % size) for i in range(size)]


def body(owners, columns, records, bin_weight):
    windows, chan, samples = records.shape
    kept = bin_weight.shape[0]
    bins = kept // 2
    spec_shape = (2, bins * 16, 128)
    even, odd, power = pl.pallas_call(
        spectra_kernel,
        in_specs=[
            pl.BlockSpec(memory_space=pltpu.HBM),
            pl.BlockSpec(memory_space=pltpu.VMEM),
        ],
        out_shape=[
            jax.ShapeDtypeStruct(spec_shape, F32),
            jax.ShapeDtypeStruct(spec_shape, F32),
            jax.ShapeDtypeStruct((windows, kept), F32),
        ],
        scratch_shapes=[
            pltpu.VMEM((windows, chan, samples), F32),
            pltpu.VMEM((windows, 2, chan, kept), F32),
            pltpu.SemaphoreType.DMA((windows,)),
        ],
        compiler_params=pltpu.CompilerParams(vmem_limit_bytes=50 << 20),
        name="spectra",
    )(records, split_tables(samples, kept))
    ahead, back, across = ring(columns, 1), ring(columns, columns - 1), ring(columns, 2)
    powers = [power] + [lax.ppermute(power, "col", p) for p in (ahead, back, across)]
    weight = bin_weight.reshape(bins, 2).T.reshape(1, kept)
    message, energy = pl.pallas_call(
        functools.partial(whiten_kernel, chan * columns),
        out_shape=[
            jax.ShapeDtypeStruct((owners, 32, chan), BF),
            jax.ShapeDtypeStruct((1, chan), F32),
        ],
        out_specs=[pl.BlockSpec(memory_space=pltpu.HBM), pl.BlockSpec(memory_space=pltpu.VMEM)],
        scratch_shapes=[
            pltpu.VMEM((owners, 32, chan), BF),
            pltpu.SemaphoreType.DMA((4,)),
        ],
        compiler_params=pltpu.CompilerParams(vmem_limit_bytes=10 << 20),
        name="whiten",
    )(even, odd, *powers, weight)

    mine = lax.all_to_all(message, "wa", split_axis=0, concat_axis=0, tiled=True)
    energies = jnp.concatenate(
        [energy] + [lax.ppermute(energy, "col", p) for p in (back, ahead, across)], axis=0
    )

    def fold(value, step):
        return value + lax.ppermute(value, "wa", [(i, i ^ step) for i in range(owners)])

    for step in (1, 2, 4):
        energies = fold(energies, step)
    mine, energies = lax.optimization_barrier((mine, energies))

    half = owners // 2
    left_a = lax.ppermute(mine[:half], "col", ahead)
    right_b = lax.ppermute(mine[half:], "col", back)
    energies = fold(energies, 8)
    late, energies = lax.optimization_barrier((mine, energies))
    left_b = lax.ppermute(late[half:], "col", ahead)
    right_a = lax.ppermute(late[:half], "col", back)
    energies = fold(energies, 16)
    left_a, right_b, energies = lax.optimization_barrier((left_a, right_b, energies))
    far_a = lax.ppermute(left_a, "col", ahead)
    far_b = lax.ppermute(right_b, "col", back)
    energies = fold(energies, 32)

    col = lax.axis_index("col").astype(jnp.int32)[None]
    scale = math.sqrt(windows * owners) * kept
    out_shape = jax.ShapeDtypeStruct((2, 2, chan, chan * columns), F32)
    lhs_shape = (2, 2 * chan, 16 * owners)

    def where(s, c):
        shift = jnp.where(s == 2, 3, jnp.where(s == 3, 2, s))
        return lax.rem(c[0] + shift, columns)

    def bin_block(count):
        return pl.BlockSpec((count, 16, chan), lambda b, s, c: (0, b, 0))

    def out_block(first):
        return pl.BlockSpec((2, 1, chan, chan), lambda b, s, c: (0, b, 0, where(s + first, c)))

    energy_block = pl.BlockSpec((columns, chan), lambda b, s, c: (0, 0))
    lhs_block = pl.BlockSpec((1,) + lhs_shape[1:], lambda b, s, c: (b, 0, 0))
    params = pltpu.CompilerParams(vmem_limit_bytes=16 << 20)
    out, lhs = pl.pallas_call(
        functools.partial(gram_near_kernel, scale),
        grid_spec=pltpu.PrefetchScalarGridSpec(
            num_scalar_prefetch=1,
            grid=(2, 3),
            in_specs=[bin_block(owners)] + [bin_block(half)] * 4 + [energy_block],
            out_specs=[out_block(0), lhs_block],
        ),
        out_shape=[out_shape, jax.ShapeDtypeStruct(lhs_shape, BF)],
        compiler_params=params,
        cost_estimate=pl.CostEstimate(
            flops=24 * chan * chan * 16 * owners, bytes_accessed=8 << 20, transcendentals=0
        ),
        name="gram_near",
    )(col, mine, right_a, right_b, left_a, left_b, energies)
    return pl.pallas_call(
        functools.partial(gram_far_kernel, scale),
        grid_spec=pltpu.PrefetchScalarGridSpec(
            num_scalar_prefetch=1,
            grid=(2, 1),
            in_specs=[pl.BlockSpec(memory_space=pltpu.VMEM)] * 3
            + [energy_block, pl.BlockSpec(memory_space=pl.ANY)],
            out_specs=out_block(3),
        ),
        out_shape=out_shape,
        input_output_aliases={5: 0},
        compiler_params=params,
        cost_estimate=pl.CostEstimate(
            flops=8 * chan * chan * 16 * owners, bytes_accessed=4 << 20, transcendentals=0
        ),
        name="gram_far",
    )(col, lhs, far_a, far_b, energies, out)


def solution(mesh):
    owners, columns = mesh.shape["wa"], mesh.shape["col"]
    return jax.shard_map(
        functools.partial(body, owners, columns),
        mesh=mesh,
        in_specs=(P("wa", "col", None), P()),
        out_specs=P(None, "wa", "col", None),
        check_vma=False,
    )
```

```python
import functools
import math

import jax
import jax.numpy as jnp
import numpy as np
from jax import lax
from jax.experimental import pallas as pl
from jax.experimental.pallas import tpu as pltpu
from jax.sharding import PartitionSpec as P

K0 = 32
BF = jnp.bfloat16
F32 = jnp.float32


def split_tables(samples, kept):
    half = samples // 2
    steps = np.arange(half, dtype=np.int64)
    tables = []
    for parity in range(2):
        freqs = K0 + np.arange(parity, kept, 2)
        angles = 2.0 * math.pi / samples * ((steps[:, None] * freqs[None, :]) % samples)
        exact = np.concatenate([np.cos(angles), -np.sin(angles)], axis=1).astype(np.float32)
        high = exact.astype(BF)
        low = (exact - high.astype(np.float32)).astype(BF)
        tables.append(np.concatenate([high, low], axis=1))
    return np.stack(tables)


def dot(a, b):
    return jnp.dot(a, b, preferred_element_type=F32)


def spectra_kernel(records, tables, results, power, held, arrived):
    windows, _, samples = records.shape
    half = samples // 2
    kept = tables.shape[2] // 2
    bins = kept // 2

    def fetch(w):
        return pltpu.make_async_copy(records.at[w], held.at[w], arrived.at[w])

    for w in range(windows):
        fetch(w).start()
    steps = lax.broadcasted_iota(jnp.int32, (1, samples), 1).astype(F32)
    taper = 0.5 - 0.5 * jnp.cos(steps * (2.0 * math.pi / samples))

    chan = records.shape[1]
    for pair in range(0, windows, 2):
        fetch(pair).wait()
        fetch(pair + 1).wait()
        tapered = held[pair : pair + 2].reshape(2 * chan, samples) * taper
        first, second = tapered[:, :half], tapered[:, half:]
        rows = [[], []]
        for parity in range(2):
            folded = first + second if parity == 0 else first - second
            high = folded.astype(BF)
            low = (folded - high.astype(F32)).astype(BF)
            both = dot(high, tables[parity])
            result = both[:, :kept] + both[:, kept:] + dot(low, tables[parity, :, :kept])
            square = result * result
            for i in range(2):
                part = slice(i * chan, i * chan + chan)
                results[pair + i, parity] = result[part]
                total = jnp.sum(square[part], axis=0, keepdims=True)
                rows[i].append(total[:, :bins] + total[:, bins:])
        for i in range(2):
            power[pair + i : pair + i + 1, :] = jnp.concatenate(rows[i], axis=1)


def turn_kernel(results, even, odd):
    windows, _, _, kept = results.shape
    bins = kept // 2
    for w in range(windows):
        for parity, spec in enumerate((even, odd)):
            turned = jnp.transpose(results[w, parity])
            for side in range(2):
                lanes = slice(128 * side, 128 * side + 128)
                spec[side, pl.ds(w, bins, stride=16), :] = turned[:bins, lanes]
                spec[side, pl.ds(8 + w, bins, stride=16), :] = turned[bins:, lanes]


def whiten_kernel(channels, even, odd, p0, p1, p2, p3, weight, message, energy, held, sent):
    bins = p0.shape[1] // 2
    group = bins // 4
    power = (p0[...] + p1[...]) + (p2[...] + p3[...])
    factor = weight[...] / jnp.sqrt(power / channels + 1e-06)
    total = jnp.zeros((8, 256), F32)

    def send(part):
        owners = pl.ds(part * group, group)
        return pltpu.make_async_copy(held.at[owners], message.at[owners], sent.at[part])

    for owner in range(bins):
        for parity, spec in enumerate((even, odd)):
            lane = parity * bins + owner
            scale = factor[:, lane : lane + 1]
            start = owner * 16
            block = jnp.concatenate(
                [spec[0, start : start + 16, :], spec[1, start : start + 16, :]], axis=1
            )
            real = (block[:8] * scale).astype(BF).astype(F32)
            imag = (block[8:] * scale).astype(BF).astype(F32)
            total = total + (real * real + imag * imag)
            held[owner, parity * 16 : parity * 16 + 16, :] = jnp.concatenate(
                [real, imag], axis=0
            ).astype(BF)
        if owner % group == group - 1:
            send(owner // group).start()
    energy[...] = jnp.sum(total, axis=0, keepdims=True)
    for part in range(4):
        send(part).wait()


def flat(block):
    return block.reshape(block.shape[0] * block.shape[1], block.shape[2])


def left_side(own, lhs):
    chan = own.shape[2]
    turned = jnp.concatenate([own[:, 8:, :], -own[:, :8, :]], axis=1)
    lhs[:chan] = jnp.transpose(flat(own[...]))
    lhs[chan:] = jnp.transpose(flat(turned))


def emit(product, energy, which, scale, out):
    chan = product.shape[1]
    rows = lax.rsqrt(energy[0:1, :]) * scale
    cols = lax.rsqrt(energy[pl.ds(which, 1), :])
    weight = jnp.transpose(jnp.broadcast_to(rows, (8, chan)))[:, :1] * cols
    out[0, 0] = product[:chan] * weight
    out[1, 0] = product[chan:] * weight


def gram_near_kernel(scale, col, own, right_a, right_b, left_a, left_b, energy, out, lhs):
    step = pl.program_id(1)
    half = lhs.shape[2] // 2

    @pl.when(step == 0)
    def _():
        left_side(own, lhs.at[0])
        emit(dot(lhs[0], flat(own[...])), energy, 0, scale, out)

    for which, first, second in ((1, right_a, right_b), (2, left_a, left_b)):

        @pl.when(step == which)
        def _():
            product = dot(lhs[0, :, :half], flat(first[...]))
            product += dot(lhs[0, :, half:], flat(second[...]))
            emit(product, energy, which, scale, out)


def gram_far_kernel(scale, col, lhs, far_a, far_b, energy, kept, out):
    half = lhs.shape[2] // 2
    b = pl.program_id(0)
    rows = pl.ds(pl.multiple_of(b * 16, 16), 16)
    product = dot(lhs[b, :, :half], flat(far_a[:, rows, :]))
    product += dot(lhs[b, :, half:], flat(far_b[:, rows, :]))
    emit(product, energy, 3, scale, out)


def ring(size, shift):
    return [(i, (i + shift) % size) for i in range(size)]


def body(owners, columns, records, bin_weight):
    windows, chan, samples = records.shape
    kept = bin_weight.shape[0]
    bins = kept // 2
    spec_shape = (2, bins * 16, 128)
    result_shape = (windows, 2, chan, kept)
    results, power = pl.pallas_call(
        spectra_kernel,
        in_specs=[
            pl.BlockSpec(memory_space=pltpu.HBM),
            pl.BlockSpec(memory_space=pltpu.VMEM),
        ],
        out_shape=[
            jax.ShapeDtypeStruct(result_shape, F32),
            jax.ShapeDtypeStruct((windows, kept), F32),
        ],
        scratch_shapes=[
            pltpu.VMEM((windows, chan, samples), F32),
            pltpu.SemaphoreType.DMA((windows,)),
        ],
        compiler_params=pltpu.CompilerParams(vmem_limit_bytes=50 << 20),
        name="spectra",
    )(records, split_tables(samples, kept))
    ahead, back, across = ring(columns, 1), ring(columns, columns - 1), ring(columns, 2)
    powers = [power] + [lax.ppermute(power, "col", p) for p in (ahead, back, across)]
    even, odd = pl.pallas_call(
        turn_kernel,
        out_shape=[jax.ShapeDtypeStruct(spec_shape, F32)] * 2,
        compiler_params=pltpu.CompilerParams(vmem_limit_bytes=10 << 20),
        cost_estimate=pl.CostEstimate(flops=0, bytes_accessed=6 << 20, transcendentals=0),
        name="turn",
    )(results)
    weight = bin_weight.reshape(bins, 2).T.reshape(1, kept)
    message, energy = pl.pallas_call(
        functools.partial(whiten_kernel, chan * columns),
        out_shape=[
            jax.ShapeDtypeStruct((owners, 32, chan), BF),
            jax.ShapeDtypeStruct((1, chan), F32),
        ],
        out_specs=[pl.BlockSpec(memory_space=pltpu.HBM), pl.BlockSpec(memory_space=pltpu.VMEM)],
        scratch_shapes=[
            pltpu.VMEM((owners, 32, chan), BF),
            pltpu.SemaphoreType.DMA((4,)),
        ],
        compiler_params=pltpu.CompilerParams(vmem_limit_bytes=10 << 20),
        name="whiten",
    )(even, odd, *powers, weight)

    mine = lax.all_to_all(message, "wa", split_axis=0, concat_axis=0, tiled=True)
    energies = jnp.concatenate(
        [energy] + [lax.ppermute(energy, "col", p) for p in (back, ahead, across)], axis=0
    )

    def fold(value, step):
        return value + lax.ppermute(value, "wa", [(i, i ^ step) for i in range(owners)])

    for step in (1, 2, 4):
        energies = fold(energies, step)
    mine, energies = lax.optimization_barrier((mine, energies))

    half = owners // 2
    left_a = lax.ppermute(mine[:half], "col", ahead)
    right_b = lax.ppermute(mine[half:], "col", back)
    energies = fold(energies, 8)
    late, energies = lax.optimization_barrier((mine, energies))
    left_b = lax.ppermute(late[half:], "col", ahead)
    right_a = lax.ppermute(late[:half], "col", back)
    energies = fold(energies, 16)
    left_a, right_b, energies = lax.optimization_barrier((left_a, right_b, energies))
    far_a = lax.ppermute(left_a, "col", ahead)
    far_b = lax.ppermute(right_b, "col", back)
    energies = fold(energies, 32)

    col = lax.axis_index("col").astype(jnp.int32)[None]
    scale = math.sqrt(windows * owners) * kept
    out_shape = jax.ShapeDtypeStruct((2, 2, chan, chan * columns), F32)
    lhs_shape = (2, 2 * chan, 16 * owners)

    def where(s, c):
        shift = jnp.where(s == 2, 3, jnp.where(s == 3, 2, s))
        return lax.rem(c[0] + shift, columns)

    def bin_block(count):
        return pl.BlockSpec((count, 16, chan), lambda b, s, c: (0, b, 0))

    def out_block(first):
        return pl.BlockSpec((2, 1, chan, chan), lambda b, s, c: (0, b, 0, where(s + first, c)))

    energy_block = pl.BlockSpec((columns, chan), lambda b, s, c: (0, 0))
    lhs_block = pl.BlockSpec((1,) + lhs_shape[1:], lambda b, s, c: (b, 0, 0))
    params = pltpu.CompilerParams(vmem_limit_bytes=16 << 20)
    out, lhs = pl.pallas_call(
        functools.partial(gram_near_kernel, scale),
        grid_spec=pltpu.PrefetchScalarGridSpec(
            num_scalar_prefetch=1,
            grid=(2, 3),
            in_specs=[bin_block(owners)] + [bin_block(half)] * 4 + [energy_block],
            out_specs=[out_block(0), lhs_block],
        ),
        out_shape=[out_shape, jax.ShapeDtypeStruct(lhs_shape, BF)],
        compiler_params=params,
        cost_estimate=pl.CostEstimate(
            flops=24 * chan * chan * 16 * owners, bytes_accessed=8 << 20, transcendentals=0
        ),
        name="gram_near",
    )(col, mine, right_a, right_b, left_a, left_b, energies)
    return pl.pallas_call(
        functools.partial(gram_far_kernel, scale),
        grid_spec=pltpu.PrefetchScalarGridSpec(
            num_scalar_prefetch=1,
            grid=(2, 1),
            in_specs=[pl.BlockSpec(memory_space=pltpu.VMEM)] * 3
            + [energy_block, pl.BlockSpec(memory_space=pl.ANY)],
            out_specs=out_block(3),
        ),
        out_shape=out_shape,
        input_output_aliases={5: 0},
        compiler_params=params,
        cost_estimate=pl.CostEstimate(
            flops=8 * chan * chan * 16 * owners, bytes_accessed=4 << 20, transcendentals=0
        ),
        name="gram_far",
    )(col, lhs, far_a, far_b, energies, out)


def solution(mesh):
    owners, columns = mesh.shape["wa"], mesh.shape["col"]
    return jax.shard_map(
        functools.partial(body, owners, columns),
        mesh=mesh,
        in_specs=(P("wa", "col", None), P()),
        out_specs=P(None, "wa", "col", None),
        check_vma=False,
    )
```

```python
import functools
import math

import jax
import jax.numpy as jnp
import numpy as np
from jax import lax
from jax.experimental import pallas as pl
from jax.experimental.pallas import tpu as pltpu
from jax.sharding import PartitionSpec as P

K0 = 32
BF = jnp.bfloat16
F32 = jnp.float32


def split_tables(samples, kept):
    half = samples // 2
    steps = np.arange(half, dtype=np.int64)
    tables = []
    for parity in range(2):
        freqs = K0 + np.arange(parity, kept, 2)
        angles = 2.0 * math.pi / samples * ((steps[:, None] * freqs[None, :]) % samples)
        exact = np.concatenate([np.cos(angles), -np.sin(angles)], axis=1).astype(np.float32)
        high = exact.astype(BF)
        low = (exact - high.astype(np.float32)).astype(BF)
        tables.append(np.concatenate([high, low], axis=1))
    return np.stack(tables)


def dot(a, b):
    return jnp.dot(a, b, preferred_element_type=F32)


def spectra_kernel(records, stored, results, power, held, tables, arrived):
    windows, _, samples = records.shape
    half = samples // 2
    kept = tables.shape[2] // 2
    bins = kept // 2

    def fetch(w):
        return pltpu.make_async_copy(records.at[w], held.at[w], arrived.at[w])

    table_copy = pltpu.make_async_copy(stored.at[pl.ds(0, 2)], tables, arrived.at[windows])
    fetch(0).start()
    table_copy.start()
    for w in range(1, windows):
        fetch(w).start()
    steps = lax.broadcasted_iota(jnp.int32, (1, samples), 1).astype(F32)
    taper = 0.5 - 0.5 * jnp.cos(steps * (2.0 * math.pi / samples))

    table_copy.wait()
    chan = records.shape[1]
    for pair in range(0, windows, 2):
        fetch(pair).wait()
        fetch(pair + 1).wait()
        tapered = held[pair : pair + 2].reshape(2 * chan, samples) * taper
        first, second = tapered[:, :half], tapered[:, half:]
        rows = [[], []]
        for parity in range(2):
            folded = first + second if parity == 0 else first - second
            high = folded.astype(BF)
            low = (folded - high.astype(F32)).astype(BF)
            both = dot(high, tables[parity])
            result = both[:, :kept] + both[:, kept:] + dot(low, tables[parity, :, :kept])
            square = result * result
            for i in range(2):
                part = slice(i * chan, i * chan + chan)
                results[pair + i, parity] = result[part]
                total = jnp.sum(square[part], axis=0, keepdims=True)
                rows[i].append(total[:, :bins] + total[:, bins:])
        for i in range(2):
            power[pair + i : pair + i + 1, :] = jnp.concatenate(rows[i], axis=1)


def turn_kernel(results, even, odd):
    windows, _, _, kept = results.shape
    bins = kept // 2
    for w in range(windows):
        for parity, spec in enumerate((even, odd)):
            turned = jnp.transpose(results[w, parity])
            for side in range(2):
                lanes = slice(128 * side, 128 * side + 128)
                spec[side, pl.ds(w, bins, stride=16), :] = turned[:bins, lanes]
                spec[side, pl.ds(8 + w, bins, stride=16), :] = turned[bins:, lanes]


def whiten_kernel(channels, even, odd, p0, p1, p2, p3, weight, message, energy, held, sent):
    bins = p0.shape[1] // 2
    group = bins // 4
    power = (p0[...] + p1[...]) + (p2[...] + p3[...])
    factor = weight[...] / jnp.sqrt(power / channels + 1e-06)
    total = jnp.zeros((8, 256), F32)

    def send(part):
        owners = pl.ds(part * group, group)
        return pltpu.make_async_copy(held.at[owners], message.at[owners], sent.at[part])

    for owner in range(bins):
        for parity, spec in enumerate((even, odd)):
            lane = parity * bins + owner
            scale = factor[:, lane : lane + 1]
            start = owner * 16
            block = jnp.concatenate(
                [spec[0, start : start + 16, :], spec[1, start : start + 16, :]], axis=1
            )
            real = (block[:8] * scale).astype(BF).astype(F32)
            imag = (block[8:] * scale).astype(BF).astype(F32)
            total = total + (real * real + imag * imag)
            held[owner, parity * 16 : parity * 16 + 16, :] = jnp.concatenate(
                [real, imag], axis=0
            ).astype(BF)
        if owner % group == group - 1:
            send(owner // group).start()
    energy[...] = jnp.sum(total, axis=0, keepdims=True)
    for part in range(4):
        send(part).wait()


def flat(block):
    return block.reshape(block.shape[0] * block.shape[1], block.shape[2])


def left_side(own, lhs):
    chan = own.shape[2]
    turned = jnp.concatenate([own[:, 8:, :], -own[:, :8, :]], axis=1)
    lhs[:chan] = jnp.transpose(flat(own[...]))
    lhs[chan:] = jnp.transpose(flat(turned))


def emit(product, energy, which, scale, out):
    chan = product.shape[1]
    rows = lax.rsqrt(energy[0:1, :]) * scale
    cols = lax.rsqrt(energy[pl.ds(which, 1), :])
    weight = jnp.transpose(jnp.broadcast_to(rows, (8, chan)))[:, :1] * cols
    out[0, 0] = product[:chan] * weight
    out[1, 0] = product[chan:] * weight


def gram_near_kernel(scale, col, own, right_a, right_b, left_a, left_b, energy, out, lhs):
    step = pl.program_id(1)
    half = lhs.shape[2] // 2

    @pl.when(step == 0)
    def _():
        left_side(own, lhs.at[0])
        emit(dot(lhs[0], flat(own[...])), energy, 0, scale, out)

    for which, first, second in ((1, right_a, right_b), (2, left_a, left_b)):

        @pl.when(step == which)
        def _():
            product = dot(lhs[0, :, :half], flat(first[...]))
            product += dot(lhs[0, :, half:], flat(second[...]))
            emit(product, energy, which, scale, out)


def gram_far_kernel(scale, col, lhs, far_a, far_b, energy, kept, out):
    half = lhs.shape[2] // 2
    b = pl.program_id(0)
    rows = pl.ds(pl.multiple_of(b * 16, 16), 16)
    product = dot(lhs[b, :, :half], flat(far_a[:, rows, :]))
    product += dot(lhs[b, :, half:], flat(far_b[:, rows, :]))
    emit(product, energy, 3, scale, out)


def ring(size, shift):
    return [(i, (i + shift) % size) for i in range(size)]


def body(owners, columns, records, bin_weight):
    windows, chan, samples = records.shape
    kept = bin_weight.shape[0]
    bins = kept // 2
    spec_shape = (2, bins * 16, 128)
    result_shape = (windows, 2, chan, kept)
    results, power = pl.pallas_call(
        spectra_kernel,
        in_specs=[
            pl.BlockSpec(memory_space=pltpu.HBM),
            pl.BlockSpec(memory_space=pltpu.HBM),
        ],
        out_shape=[
            jax.ShapeDtypeStruct(result_shape, F32),
            jax.ShapeDtypeStruct((windows, kept), F32),
        ],
        scratch_shapes=[
            pltpu.VMEM((windows, chan, samples), F32),
            pltpu.VMEM((2, samples // 2, 2 * kept), BF),
            pltpu.SemaphoreType.DMA((windows + 1,)),
        ],
        compiler_params=pltpu.CompilerParams(vmem_limit_bytes=51 << 20),
        name="spectra",
    )(records, np.pad(split_tables(samples, kept), ((0, 14), (0, 0), (0, 0))))
    ahead, back, across = ring(columns, 1), ring(columns, columns - 1), ring(columns, 2)
    powers = [power] + [lax.ppermute(power, "col", p) for p in (ahead, back, across)]
    even, odd = pl.pallas_call(
        turn_kernel,
        out_shape=[jax.ShapeDtypeStruct(spec_shape, F32)] * 2,
        compiler_params=pltpu.CompilerParams(vmem_limit_bytes=10 << 20),
        cost_estimate=pl.CostEstimate(flops=0, bytes_accessed=6 << 20, transcendentals=0),
        name="turn",
    )(results)
    weight = bin_weight.reshape(bins, 2).T.reshape(1, kept)
    message, energy = pl.pallas_call(
        functools.partial(whiten_kernel, chan * columns),
        out_shape=[
            jax.ShapeDtypeStruct((owners, 32, chan), BF),
            jax.ShapeDtypeStruct((1, chan), F32),
        ],
        out_specs=[pl.BlockSpec(memory_space=pltpu.HBM), pl.BlockSpec(memory_space=pltpu.VMEM)],
        scratch_shapes=[
            pltpu.VMEM((owners, 32, chan), BF),
            pltpu.SemaphoreType.DMA((4,)),
        ],
        compiler_params=pltpu.CompilerParams(vmem_limit_bytes=10 << 20),
        name="whiten",
    )(even, odd, *powers, weight)

    mine = lax.all_to_all(message, "wa", split_axis=0, concat_axis=0, tiled=True)
    energies = jnp.concatenate(
        [energy] + [lax.ppermute(energy, "col", p) for p in (back, ahead, across)], axis=0
    )

    def fold(value, step):
        return value + lax.ppermute(value, "wa", [(i, i ^ step) for i in range(owners)])

    for step in (1, 2, 4):
        energies = fold(energies, step)
    mine, energies = lax.optimization_barrier((mine, energies))

    half = owners // 2
    left_a = lax.ppermute(mine[:half], "col", ahead)
    right_b = lax.ppermute(mine[half:], "col", back)
    energies = fold(energies, 8)
    late, energies = lax.optimization_barrier((mine, energies))
    left_b = lax.ppermute(late[half:], "col", ahead)
    right_a = lax.ppermute(late[:half], "col", back)
    energies = fold(energies, 16)
    left_a, right_b, energies = lax.optimization_barrier((left_a, right_b, energies))
    far_a = lax.ppermute(left_a, "col", ahead)
    far_b = lax.ppermute(right_b, "col", back)
    energies = fold(energies, 32)

    col = lax.axis_index("col").astype(jnp.int32)[None]
    scale = math.sqrt(windows * owners) * kept
    out_shape = jax.ShapeDtypeStruct((2, 2, chan, chan * columns), F32)
    lhs_shape = (2, 2 * chan, 16 * owners)

    def where(s, c):
        shift = jnp.where(s == 2, 3, jnp.where(s == 3, 2, s))
        return lax.rem(c[0] + shift, columns)

    def bin_block(count):
        return pl.BlockSpec((count, 16, chan), lambda b, s, c: (0, b, 0))

    def out_block(first):
        return pl.BlockSpec((2, 1, chan, chan), lambda b, s, c: (0, b, 0, where(s + first, c)))

    energy_block = pl.BlockSpec((columns, chan), lambda b, s, c: (0, 0))
    lhs_block = pl.BlockSpec((1,) + lhs_shape[1:], lambda b, s, c: (b, 0, 0))
    params = pltpu.CompilerParams(vmem_limit_bytes=16 << 20)
    out, lhs = pl.pallas_call(
        functools.partial(gram_near_kernel, scale),
        grid_spec=pltpu.PrefetchScalarGridSpec(
            num_scalar_prefetch=1,
            grid=(2, 3),
            in_specs=[bin_block(owners)] + [bin_block(half)] * 4 + [energy_block],
            out_specs=[out_block(0), lhs_block],
        ),
        out_shape=[out_shape, jax.ShapeDtypeStruct(lhs_shape, BF)],
        compiler_params=params,
        cost_estimate=pl.CostEstimate(
            flops=24 * chan * chan * 16 * owners, bytes_accessed=8 << 20, transcendentals=0
        ),
        name="gram_near",
    )(col, mine, right_a, right_b, left_a, left_b, energies)
    return pl.pallas_call(
        functools.partial(gram_far_kernel, scale),
        grid_spec=pltpu.PrefetchScalarGridSpec(
            num_scalar_prefetch=1,
            grid=(2, 1),
            in_specs=[pl.BlockSpec(memory_space=pltpu.VMEM)] * 3
            + [energy_block, pl.BlockSpec(memory_space=pl.ANY)],
            out_specs=out_block(3),
        ),
        out_shape=out_shape,
        input_output_aliases={5: 0},
        compiler_params=params,
        cost_estimate=pl.CostEstimate(
            flops=8 * chan * chan * 16 * owners, bytes_accessed=4 << 20, transcendentals=0
        ),
        name="gram_far",
    )(col, lhs, far_a, far_b, energies, out)


def solution(mesh):
    owners, columns = mesh.shape["wa"], mesh.shape["col"]
    return jax.shard_map(
        functools.partial(body, owners, columns),
        mesh=mesh,
        in_specs=(P("wa", "col", None), P()),
        out_specs=P(None, "wa", "col", None),
        check_vma=False,
    )
```

```python
import functools
import math

import jax
import jax.numpy as jnp
import numpy as np
from jax import lax
from jax.experimental import pallas as pl
from jax.experimental.pallas import tpu as pltpu
from jax.sharding import PartitionSpec as P

K0 = 32
BF = jnp.bfloat16
F32 = jnp.float32


def split_tables(samples, kept):
    half = samples // 2
    steps = np.arange(half, dtype=np.int64)
    tables = []
    for parity in range(2):
        freqs = K0 + np.arange(parity, kept, 2)
        angles = 2.0 * math.pi / samples * ((steps[:, None] * freqs[None, :]) % samples)
        exact = np.concatenate([np.cos(angles), -np.sin(angles)], axis=1).astype(np.float32)
        high = exact.astype(BF)
        low = (exact - high.astype(np.float32)).astype(BF)
        tables.append(np.concatenate([high, low], axis=1))
    return np.stack(tables)


def dot(a, b):
    return jnp.dot(a, b, preferred_element_type=F32)


def spectra_kernel(records, stored, results, power, held, tables, arrived):
    windows, _, samples = records.shape
    half = samples // 2
    kept = tables.shape[2] // 2
    bins = kept // 2

    def fetch(w):
        return pltpu.make_async_copy(records.at[w], held.at[w], arrived.at[w])

    table_copy = pltpu.make_async_copy(stored.at[pl.ds(0, 2)], tables, arrived.at[windows])
    fetch(0).start()
    table_copy.start()
    for w in range(1, windows):
        fetch(w).start()
    steps = lax.broadcasted_iota(jnp.int32, (1, samples), 1).astype(F32)
    taper = 0.5 - 0.5 * jnp.cos(steps * (2.0 * math.pi / samples))

    table_copy.wait()
    chan = records.shape[1]
    pairs = [(w, 2) for w in range(0, windows - 2, 2)]
    for pair, count in pairs + [(windows - 2, 1), (windows - 1, 1)]:
        for i in range(count):
            fetch(pair + i).wait()
        tapered = held[pair : pair + count].reshape(count * chan, samples) * taper
        first, second = tapered[:, :half], tapered[:, half:]
        rows = [[] for _ in range(count)]
        for parity in range(2):
            folded = first + second if parity == 0 else first - second
            high = folded.astype(BF)
            low = (folded - high.astype(F32)).astype(BF)
            both = dot(high, tables[parity])
            result = both[:, :kept] + both[:, kept:] + dot(low, tables[parity, :, :kept])
            square = result * result
            for i in range(count):
                part = slice(i * chan, i * chan + chan)
                results[pair + i, parity] = result[part]
                total = jnp.sum(square[part], axis=0, keepdims=True)
                rows[i].append(total[:, :bins] + total[:, bins:])
        for i in range(count):
            power[pair + i : pair + i + 1, :] = jnp.concatenate(rows[i], axis=1)


def turn_kernel(results, even, odd):
    windows, _, _, kept = results.shape
    bins = kept // 2
    for w in range(windows):
        for parity, spec in enumerate((even, odd)):
            turned = jnp.transpose(results[w, parity])
            for side in range(2):
                lanes = slice(128 * side, 128 * side + 128)
                spec[side, pl.ds(w, bins, stride=16), :] = turned[:bins, lanes]
                spec[side, pl.ds(8 + w, bins, stride=16), :] = turned[bins:, lanes]


def whiten_kernel(channels, even, odd, p0, p1, p2, p3, weight, message, energy, held, sent):
    bins = p0.shape[1] // 2
    group = bins // 4
    power = (p0[...] + p1[...]) + (p2[...] + p3[...])
    factor = weight[...] / jnp.sqrt(power / channels + 1e-06)
    total = jnp.zeros((8, 256), F32)

    def send(part):
        owners = pl.ds(part * group, group)
        return pltpu.make_async_copy(held.at[owners], message.at[owners], sent.at[part])

    for owner in range(bins):
        for parity, spec in enumerate((even, odd)):
            lane = parity * bins + owner
            scale = factor[:, lane : lane + 1]
            start = owner * 16
            block = jnp.concatenate(
                [spec[0, start : start + 16, :], spec[1, start : start + 16, :]], axis=1
            )
            real = (block[:8] * scale).astype(BF).astype(F32)
            imag = (block[8:] * scale).astype(BF).astype(F32)
            total = total + (real * real + imag * imag)
            held[owner, parity * 16 : parity * 16 + 16, :] = jnp.concatenate(
                [real, imag], axis=0
            ).astype(BF)
        if owner % group == group - 1:
            send(owner // group).start()
    energy[...] = jnp.sum(total, axis=0, keepdims=True)
    for part in range(4):
        send(part).wait()


def flat(block):
    return block.reshape(block.shape[0] * block.shape[1], block.shape[2])


def left_side(own, lhs):
    chan = own.shape[2]
    turned = jnp.concatenate([own[:, 8:, :], -own[:, :8, :]], axis=1)
    lhs[:chan] = jnp.transpose(flat(own[...]))
    lhs[chan:] = jnp.transpose(flat(turned))


def emit(product, energy, which, scale, out):
    chan = product.shape[1]
    rows = lax.rsqrt(energy[0:1, :]) * scale
    cols = lax.rsqrt(energy[pl.ds(which, 1), :])
    weight = jnp.transpose(jnp.broadcast_to(rows, (8, chan)))[:, :1] * cols
    out[0, 0] = product[:chan] * weight
    out[1, 0] = product[chan:] * weight


def gram_near_kernel(scale, col, own, right_a, right_b, left_a, left_b, energy, out, lhs):
    step = pl.program_id(1)
    half = lhs.shape[2] // 2

    @pl.when(step == 0)
    def _():
        left_side(own, lhs.at[0])
        emit(dot(lhs[0], flat(own[...])), energy, 0, scale, out)

    for which, first, second in ((1, right_a, right_b), (2, left_a, left_b)):

        @pl.when(step == which)
        def _():
            product = dot(lhs[0, :, :half], flat(first[...]))
            product += dot(lhs[0, :, half:], flat(second[...]))
            emit(product, energy, which, scale, out)


def gram_far_kernel(scale, col, lhs, far_a, far_b, energy, kept, out):
    half = lhs.shape[2] // 2
    b = pl.program_id(0)
    rows = pl.ds(pl.multiple_of(b * 16, 16), 16)
    product = dot(lhs[b, :, :half], flat(far_a[:, rows, :]))
    product += dot(lhs[b, :, half:], flat(far_b[:, rows, :]))
    emit(product, energy, 3, scale, out)


def ring(size, shift):
    return [(i, (i + shift) % size) for i in range(size)]


def body(owners, columns, records, bin_weight):
    windows, chan, samples = records.shape
    kept = bin_weight.shape[0]
    bins = kept // 2
    spec_shape = (2, bins * 16, 128)
    result_shape = (windows, 2, chan, kept)
    results, power = pl.pallas_call(
        spectra_kernel,
        in_specs=[
            pl.BlockSpec(memory_space=pltpu.HBM),
            pl.BlockSpec(memory_space=pltpu.HBM),
        ],
        out_shape=[
            jax.ShapeDtypeStruct(result_shape, F32),
            jax.ShapeDtypeStruct((windows, kept), F32),
        ],
        scratch_shapes=[
            pltpu.VMEM((windows, chan, samples), F32),
            pltpu.VMEM((2, samples // 2, 2 * kept), BF),
            pltpu.SemaphoreType.DMA((windows + 1,)),
        ],
        compiler_params=pltpu.CompilerParams(vmem_limit_bytes=51 << 20),
        name="spectra",
    )(records, np.pad(split_tables(samples, kept), ((0, 14), (0, 0), (0, 0))))
    ahead, back, across = ring(columns, 1), ring(columns, columns - 1), ring(columns, 2)
    powers = [power] + [lax.ppermute(power, "col", p) for p in (ahead, back, across)]
    even, odd = pl.pallas_call(
        turn_kernel,
        out_shape=[jax.ShapeDtypeStruct(spec_shape, F32)] * 2,
        compiler_params=pltpu.CompilerParams(vmem_limit_bytes=10 << 20),
        cost_estimate=pl.CostEstimate(flops=0, bytes_accessed=6 << 20, transcendentals=0),
        name="turn",
    )(results)
    weight = bin_weight.reshape(bins, 2).T.reshape(1, kept)
    message, energy = pl.pallas_call(
        functools.partial(whiten_kernel, chan * columns),
        out_shape=[
            jax.ShapeDtypeStruct((owners, 32, chan), BF),
            jax.ShapeDtypeStruct((1, chan), F32),
        ],
        out_specs=[pl.BlockSpec(memory_space=pltpu.HBM), pl.BlockSpec(memory_space=pltpu.VMEM)],
        scratch_shapes=[
            pltpu.VMEM((owners, 32, chan), BF),
            pltpu.SemaphoreType.DMA((4,)),
        ],
        compiler_params=pltpu.CompilerParams(vmem_limit_bytes=10 << 20),
        name="whiten",
    )(even, odd, *powers, weight)

    mine = lax.all_to_all(message, "wa", split_axis=0, concat_axis=0, tiled=True)
    energies = jnp.concatenate(
        [energy] + [lax.ppermute(energy, "col", p) for p in (back, ahead, across)], axis=0
    )

    def fold(value, step):
        return value + lax.ppermute(value, "wa", [(i, i ^ step) for i in range(owners)])

    for step in (1, 2, 4):
        energies = fold(energies, step)
    mine, energies = lax.optimization_barrier((mine, energies))

    half = owners // 2
    left_a = lax.ppermute(mine[:half], "col", ahead)
    right_b = lax.ppermute(mine[half:], "col", back)
    energies = fold(energies, 8)
    late, energies = lax.optimization_barrier((mine, energies))
    left_b = lax.ppermute(late[half:], "col", ahead)
    right_a = lax.ppermute(late[:half], "col", back)
    energies = fold(energies, 16)
    left_a, right_b, energies = lax.optimization_barrier((left_a, right_b, energies))
    far_a = lax.ppermute(left_a, "col", ahead)
    far_b = lax.ppermute(right_b, "col", back)
    energies = fold(energies, 32)

    col = lax.axis_index("col").astype(jnp.int32)[None]
    scale = math.sqrt(windows * owners) * kept
    out_shape = jax.ShapeDtypeStruct((2, 2, chan, chan * columns), F32)
    lhs_shape = (2, 2 * chan, 16 * owners)

    def where(s, c):
        shift = jnp.where(s == 2, 3, jnp.where(s == 3, 2, s))
        return lax.rem(c[0] + shift, columns)

    def bin_block(count):
        return pl.BlockSpec((count, 16, chan), lambda b, s, c: (0, b, 0))

    def out_block(first):
        return pl.BlockSpec((2, 1, chan, chan), lambda b, s, c: (0, b, 0, where(s + first, c)))

    energy_block = pl.BlockSpec((columns, chan), lambda b, s, c: (0, 0))
    lhs_block = pl.BlockSpec((1,) + lhs_shape[1:], lambda b, s, c: (b, 0, 0))
    params = pltpu.CompilerParams(vmem_limit_bytes=16 << 20)
    out, lhs = pl.pallas_call(
        functools.partial(gram_near_kernel, scale),
        grid_spec=pltpu.PrefetchScalarGridSpec(
            num_scalar_prefetch=1,
            grid=(2, 3),
            in_specs=[bin_block(owners)] + [bin_block(half)] * 4 + [energy_block],
            out_specs=[out_block(0), lhs_block],
        ),
        out_shape=[out_shape, jax.ShapeDtypeStruct(lhs_shape, BF)],
        compiler_params=params,
        cost_estimate=pl.CostEstimate(
            flops=24 * chan * chan * 16 * owners, bytes_accessed=8 << 20, transcendentals=0
        ),
        name="gram_near",
    )(col, mine, right_a, right_b, left_a, left_b, energies)
    return pl.pallas_call(
        functools.partial(gram_far_kernel, scale),
        grid_spec=pltpu.PrefetchScalarGridSpec(
            num_scalar_prefetch=1,
            grid=(2, 1),
            in_specs=[pl.BlockSpec(memory_space=pltpu.VMEM)] * 3
            + [energy_block, pl.BlockSpec(memory_space=pl.ANY)],
            out_specs=out_block(3),
        ),
        out_shape=out_shape,
        input_output_aliases={5: 0},
        compiler_params=params,
        cost_estimate=pl.CostEstimate(
            flops=8 * chan * chan * 16 * owners, bytes_accessed=4 << 20, transcendentals=0
        ),
        name="gram_far",
    )(col, lhs, far_a, far_b, energies, out)


def solution(mesh):
    owners, columns = mesh.shape["wa"], mesh.shape["col"]
    return jax.shard_map(
        functools.partial(body, owners, columns),
        mesh=mesh,
        in_specs=(P("wa", "col", None), P()),
        out_specs=P(None, "wa", "col", None),
        check_vma=False,
    )
```
